1024 devices in a mesh: dp: 64 (over x, z_lo, core), node: 16 (over y, z_hi).
Axes of the slice: x: 4, y: 8, z: 16 (z_hi: 2, z_lo: 8; z = z_hi * 8 + z_lo), core: 2. Of those that a mesh axis runs over, the one named last changes fastest.
Arguments:
- tokens: bfloat16 [16384, 12288], P('dp', 'node'), may hold values from -16 to 16
- key_weight: bfloat16 [1024, 12288], P('dp', 'node'), may hold values from -0.0546875 to 0.0546875
- key_cotangent: bfloat16 [16384, 1024], P(('dp', 'node')), may hold values from -24 to 24
Outputs:
- keys: bfloat16 [16384, 1024], P(('dp', 'node'))
- token_grad: bfloat16 [16384, 12288], P('dp', 'node')
- weight_grad: float32 [1024, 12288], P('dp', 'node')
The draws below stay inside these ranges and needn't reach their ends.
All inputs are finite; a program needn't handle non-finite values.
Results may differ from the reference program's by a relative error of at most 0.0015.
Values may be sent and summed in bfloat16 or wider, within the bound.
A program may use at most 32 MiB of HBM per device.

```python
import jax
import jax.numpy as jnp

D = 12288
KVW = 1024
TOKENS = 16384
REPLICAS = 64


def spiked(drawn, rng, source, target, blocks, factor):
    def block_of(position):
        return (jnp.arange(drawn.shape[position]) // (drawn.shape[position] // blocks)).reshape((-1,) + (1,) * (drawn.ndim - 1 - position))

    first = jax.random.permutation(rng, blocks)[block_of(target)]
    far = (block_of(target) + blocks // 2) % blocks
    return jnp.where((block_of(source) == first) | (block_of(source) == far), factor * drawn, drawn)


def level_of(own_key, extent, pieces, low, largest):
    def one(position, blocks):
        heights = jax.random.uniform(jax.random.fold_in(jax.random.fold_in(own_key, 6), position), (blocks,), jnp.float32, low / len(pieces), largest / len(pieces))
        return jnp.repeat(jnp.exp(heights), extent[position] // blocks).reshape((-1,) + (1,) * (len(extent) - position - 1))

    gain = one(*pieces[0])
    for cut in pieces[1:]:
        gain = gain * one(*cut)
    return gain


def scatter_about(stream_key, extent, width, reach, shards=(), held_as=jnp.bfloat16):
    result = jax.random.normal(stream_key, extent, jnp.float32) * width
    if len(shards) > 0:
        result = level_of(stream_key, extent, shards, -0.22, 0.18) * result
    return jnp.clip(result, min=-reach, max=reach).astype(held_as)


def noise_with(key, shape, width, limit, split, heavy, kind=jnp.bfloat16):
    result = width * jax.random.normal(key, shape, jnp.float32)
    if split:
        result = result * level_of(key, shape, split, -0.22, 0.18)
    return jnp.clip(spiked(result, jax.random.fold_in(key, 3), *heavy), -limit, limit).astype(kind)


def setup_inputs(seed: int = 0) -> dict:
    key_list = jax.random.split(jax.random.key(seed), 4)
    tokens = noise_with(key_list[0], (TOKENS, D), 1.0, 16.0, ((0, 64), (1, 16)), (1, 0, 64, 4.0))
    key_weight = scatter_about(key_list[1], (KVW, D), D ** -0.5, 0.0546875, ((0, 64), (1, 16)))
    key_cotangent = noise_with(key_list[2], (TOKENS, KVW), 1.0, 24.0, ((0, 1024),), (0, 1, 1024, 6.0))
    return {"tokens": tokens, "key_weight": key_weight, "key_cotangent": key_cotangent}


def reference(tokens, key_weight, key_cotangent):
    keys = jnp.dot(tokens, key_weight.T, preferred_element_type=jnp.float32).astype(jnp.bfloat16)
    token_grad = jnp.dot(key_cotangent, key_weight, preferred_element_type=jnp.float32).astype(jnp.bfloat16)
    weight_grad = jnp.dot(key_cotangent.T, tokens, preferred_element_type=jnp.float32) / REPLICAS
    return keys, token_grad, weight_grad
```

```python
import jax
import jax.numpy as jnp
from jax import lax
from jax.experimental import pallas as pl
from jax.experimental.pallas import tpu as pltpu
from jax.sharding import PartitionSpec as P

MESH = pl.DeviceIdType.MESH
NX, NZ, NC, NY, NH = 4, 8, 2, 8, 2
D, KV, T = 768, 1024, 256
HALF = D // 2
FAR_FIRST = (4, 3, 5, 2, 6, 1, 7)

f32, bf16 = jnp.float32, jnp.bfloat16

KEY_SCALE = 2.0**11
WX_SCALE = 2.0**24
WZ_SCALE = 2.0**22


def cube(value, scale):
    value = value * scale
    return (value * value * value).astype(bf16)


def uncube(sent, scale):
    sent = sent.astype(f32)
    root = jnp.exp(jnp.log(jnp.abs(sent)) * (1.0 / 3.0)) * (1.0 / scale)
    return jnp.where(sent < 0, -root, root)


def sixth(value, scale):
    value = value * scale
    value = value * value * value
    return (value * jnp.abs(value)).astype(bf16)


def unsixth(sent, scale):
    sent = sent.astype(f32)
    root = jnp.exp(jnp.log(jnp.abs(sent)) * (1.0 / 6.0)) * (1.0 / scale)
    return jnp.where(sent < 0, -root, root)


def dot(left, right, dims):
    return lax.dot_general(left, right, (dims, ((), ())), preferred_element_type=f32)


def kernel(
    tok, wsh, csh, keys, tgrad, wgrad,
    wbuf, cown, coth, toth, wsend, wrecv, wsum, zsend, zrecv, ksend, krecv, kpart, kz, kzr, ss, rs,
):
    dp, node = lax.axis_index("dp"), lax.axis_index("node")
    x, zl, c = dp // 16, lax.rem(dp // 2, 8), lax.rem(dp, 2)
    y, zh = node // 2, lax.rem(node, 2)
    oc, oh = 1 - c, 1 - zh

    def at(px=x, pz=zl, pc=c, py=y, ph=zh):
        return ((px * NZ + pz) * NC + pc, py * NH + ph)

    def xk(k):
        return lax.rem(x + k, NX)

    def zk(k):
        return lax.rem(zl + k, NZ)

    def yk(k):
        return lax.rem(y + k, NY)

    barrier = pltpu.get_barrier_semaphore()
    peers = [at(ph=oh), at(pc=oc)]
    peers += [at(pz=zk(k)) for k in range(1, NZ)]
    peers += [at(pz=zk(k), pc=oc) for k in range(1, NZ)]
    peers += [at(py=yk(k)) for k in range(1, NY)]
    peers += [at(px=xk(k)) for k in range(1, NX)]
    for peer in peers:
        pl.semaphore_signal(barrier, inc=1, device_id=peer, device_id_type=MESH)

    cown[y, zh] = csh[...]
    wbuf[x, zl, c] = wsh[...]
    pl.semaphore_wait(barrier, len(peers))

    started = []

    def send(src, dst, peer):
        index = len(started)
        copy = pltpu.make_async_remote_copy(
            src_ref=src, dst_ref=dst, send_sem=ss.at[index], recv_sem=rs.at[index], device_id=peer, device_id_type=MESH
        )
        copy.start()
        started.append(copy)
        return copy

    def arrived(copies):
        for copy in copies:
            copy.wait_recv()

    cot_z = send(csh, cown.at[y, zh], at(ph=oh))
    cot_y = [send(csh, cown.at[y, zh], at(py=yk(k))) for k in FAR_FIRST]
    w_z = [send(wsh, wbuf.at[x, zl, c], at(pz=zk(k))) for k in FAR_FIRST]
    tok_c = send(tok.at[:, pl.ds(pl.multiple_of(oc * HALF, 128), HALF)], toth, at(pc=oc))

    arrived(cot_y)
    cot_c = [send(cown.at[:, zh], coth.at[:, zh], at(pc=oc))]
    cot_z.wait_recv()
    cot_y = [send(cown.at[y, oh], cown.at[y, oh], at(py=yk(k))) for k in FAR_FIRST]
    arrived(w_z)
    w_x = [(k, send(wbuf.at[x, :, c], wbuf.at[x, :, c], at(px=xk(k)))) for k in (2, 1, 3)]
    w_c = [(x, send(wbuf.at[x, :, c], wbuf.at[x, :, c], at(pc=oc)))]
    arrived(cot_y)
    cot_c.append(send(cown.at[:, oh], coth.at[:, oh], at(pc=oc)))

    tok_c.wait_recv()
    arrived(cot_c)
    mine = tok[:, pl.ds(pl.multiple_of(c * HALF, 128), HALF)]

    def weight_term(block):
        columns = pl.ds(pl.multiple_of(block * 256, 256), 256)
        return dot(cown[:, :, :, columns].reshape(T, 256), mine, ((0,), (0,))) + dot(
            coth[:, :, :, columns].reshape(T, 256), toth[...], ((0,), (0,))
        )

    wg_x = []
    for slot, k in enumerate((2, 1, 3)):
        wsend[slot] = cube(weight_term(xk(k)), WX_SCALE)
        wg_x.append(send(wsend.at[slot], wrecv.at[slot], at(px=xk(k))))
    own_term = weight_term(x)

    def key_block(slot, block):
        weight = wbuf[block].reshape(256, D)
        term = dot(tok[...], weight, ((1,), (1,)))
        kpart[slot] = term.reshape(NY, 32, 256)
        ksend[slot] = sixth(term, KEY_SCALE).reshape(NY, 32, 256)
        return [send(ksend.at[slot, yk(k)], krecv.at[slot, i], at(py=yk(k))) for i, k in enumerate(FAR_FIRST)]

    w_c[0][1].wait_recv()
    k_y = [key_block(0, x)]
    for k, copy in w_x:
        copy.wait_recv()
        source = xk(NX - k)
        w_c.append((source, send(wbuf.at[source, :, c], wbuf.at[source, :, c], at(pc=oc))))
    for slot in range(1, NX):
        source, copy = w_c[slot]
        copy.wait_recv()
        k_y.append(key_block(slot, source))

    arrived(wg_x)
    total = own_term
    for slot in range(3):
        total = total + uncube(wrecv[slot], WX_SCALE)
    wsum[...] = total.reshape(NZ, NC, 16, HALF)
    zsend[...] = cube(total, WZ_SCALE).reshape(NZ, NC, 16, HALF)
    wg_z = []
    for i, k in enumerate(FAR_FIRST):
        wg_z.append(send(zsend.at[zk(k), c], zrecv.at[0, i], at(pz=zk(k))))
        wg_z.append(send(zsend.at[zk(k), oc], zrecv.at[1, i], at(pz=zk(k), pc=oc)))
    wg_z.append(send(zsend.at[zl, oc], zrecv.at[1, 7], at(pc=oc)))

    grad = jnp.zeros((T, D), f32)
    for block in range(NX):
        grad = grad + dot(
            cown[:, :, :, block * 256 : (block + 1) * 256].reshape(T, 256), wbuf[block].reshape(256, D), ((1,), (0,))
        )
    tgrad[...] = grad.astype(bf16)

    k_z = []
    for slot in range(NX):
        arrived(k_y[slot])
        rows = kpart[slot, y]
        for i in range(NY - 1):
            rows = rows + unsixth(krecv[slot, i], KEY_SCALE)
        kz[slot] = rows.reshape(NH, 16, 256)
        k_z.append(send(kz.at[slot, oh], kzr.at[slot], at(ph=oh)))

    arrived(wg_z)
    for core in range(NC):
        if core == 0:
            rows = wsum[zl, c]
        else:
            rows = uncube(zrecv[1, 7], WZ_SCALE)
        for i in range(NZ - 1):
            rows = rows + uncube(zrecv[core, i], WZ_SCALE)
        half = c if core == 0 else oc
        wgrad[:, pl.ds(pl.multiple_of(half * HALF, 128), HALF)] = rows * (1.0 / 64)

    for slot in range(NX):
        k_z[slot].wait_recv()
        block = x if slot == 0 else w_c[slot][0]
        columns = pl.ds(pl.multiple_of(block * 256, 256), 256)
        keys[:, columns] = (kz[slot, zh] + kzr[slot]).astype(bf16)

    for copy in started:
        copy.wait_send()


COPIES = 1 + 7 + 7 + 1 + 1 + 7 + 3 + 1 + 1 + 3 + 7 + 3 + 21 + 15 + 4


def body(tokens, key_weight, key_cotangent):
    vmem = pl.BlockSpec(memory_space=pltpu.VMEM)
    return pl.pallas_call(
        kernel,
        out_shape=(
            jax.ShapeDtypeStruct((16, KV), bf16),
            jax.ShapeDtypeStruct((T, D), bf16),
            jax.ShapeDtypeStruct((16, D), f32),
        ),
        in_specs=[vmem] * 3,
        out_specs=(vmem,) * 3,
        scratch_shapes=[
            pltpu.VMEM((NX, NZ, NC, 16, D), bf16),
            pltpu.VMEM((NY, NH, 16, KV), bf16),
            pltpu.VMEM((NY, NH, 16, KV), bf16),
            pltpu.VMEM((T, HALF), bf16),
            pltpu.VMEM((3, T, HALF), bf16),
            pltpu.VMEM((3, T, HALF), bf16),
            pltpu.VMEM((NZ, NC, 16, HALF), f32),
            pltpu.VMEM((NZ, NC, 16, HALF), bf16),
            pltpu.VMEM((2, 8, 16, HALF), bf16),
            pltpu.VMEM((NX, NY, 32, 256), bf16),
            pltpu.VMEM((NX, NY - 1, 32, 256), bf16),
            pltpu.VMEM((NX, NY, 32, 256), f32),
            pltpu.VMEM((NX, NH, 16, 256), f32),
            pltpu.VMEM((NX, 16, 256), f32),
            pltpu.SemaphoreType.DMA((COPIES,)),
            pltpu.SemaphoreType.DMA((COPIES,)),
        ],
        compiler_params=pltpu.CompilerParams(
            collective_id=0, has_side_effects=True, vmem_limit_bytes=48 * 1024 * 1024
        ),
        name="key_projection",
    )(tokens, key_weight, key_cotangent)


def solution(mesh):
    in_specs = (P("dp", "node"), P("dp", "node"), P(("dp", "node"), None))
    out_specs = (P(("dp", "node"), None), P("dp", "node"), P("dp", "node"))
    return jax.shard_map(body, mesh=mesh, in_specs=in_specs, out_specs=out_specs, check_vma=False)
```

```python
import jax
import jax.numpy as jnp
from jax import lax
from jax.experimental import pallas as pl
from jax.experimental.pallas import tpu as pltpu
from jax.sharding import PartitionSpec as P

MESH = pl.DeviceIdType.MESH
NX, NZ, NC, NY, NH = 4, 8, 2, 8, 2
D, KV, T = 768, 1024, 256
HALF = D // 2
FAR_FIRST = (4, 3, 5, 2, 6, 1, 7)

f32, bf16 = jnp.float32, jnp.bfloat16

KEY_SCALE = 2.0**11
WX_SCALE = 2.0**24
WZ_SCALE = 2.0**22


def cube(value, scale):
    value = value * scale
    return (value * value * value).astype(bf16)


def uncube(sent, scale):
    sent = sent.astype(f32)
    root = jnp.exp(jnp.log(jnp.abs(sent)) * (1.0 / 3.0)) * (1.0 / scale)
    return jnp.where(sent < 0, -root, root)


def sixth(value, scale):
    value = value * scale
    value = value * value * value
    return (value * jnp.abs(value)).astype(bf16)


def unsixth(sent, scale):
    sent = sent.astype(f32)
    root = jnp.exp(jnp.log(jnp.abs(sent)) * (1.0 / 6.0)) * (1.0 / scale)
    return jnp.where(sent < 0, -root, root)


def dot(left, right, dims):
    return lax.dot_general(left, right, (dims, ((), ())), preferred_element_type=f32)


def kernel(
    tok_in, w_in, cot_in, keys, tgrad, wgrad,
    tok, wbuf, cown, coth, toth, wsend, wrecv, wsum, zsend, zrecv, ksend, krecv, kpart, ksum, kzs, kzr, ls, ss, rs,
):
    dp, node = lax.axis_index("dp"), lax.axis_index("node")
    x, zl, c = dp // 16, lax.rem(dp // 2, 8), lax.rem(dp, 2)
    y, zh = node // 2, lax.rem(node, 2)
    oc, oh = 1 - c, 1 - zh
    quad, spot = zl // 4, lax.rem(zl, 4)
    across = lax.rem(zl + 4, NZ)

    def at(px=x, pz=zl, pc=c, py=y, ph=zh):
        return ((px * NZ + pz) * NC + pc, py * NH + ph)

    def xk(k):
        return lax.rem(x + k, NX)

    def yk(k):
        return lax.rem(y + k, NY)

    def inside(k):
        return quad * 4 + lax.rem(spot + k, 4)

    def outside(k):
        return (1 - quad) * 4 + lax.rem(spot + k, 4)

    zpeers = [outside(k) for k in range(4)] + [inside(k) for k in (1, 2, 3)]
    barrier = pltpu.get_barrier_semaphore()
    peers = [at(ph=oh)]
    peers += [at(pz=pz) for pz in zpeers]
    peers += [at(pz=pz, pc=oc) for pz in zpeers]
    peers += [at(py=yk(k)) for k in FAR_FIRST]
    peers += [at(px=xk(k)) for k in (2, 1, 3)]
    peers += [at(pc=oc)]
    for peer in peers:
        pl.semaphore_signal(barrier, inc=1, device_id=peer, device_id_type=MESH)

    fetches = [
        pltpu.make_async_copy(cot_in, cown.at[y, zh], ls.at[0]),
        pltpu.make_async_copy(w_in, wbuf.at[x, zl, c], ls.at[1]),
        pltpu.make_async_copy(tok_in, tok, ls.at[2]),
    ]
    for fetch in fetches:
        fetch.start()
    for fetch in fetches:
        fetch.wait()
    pl.semaphore_wait(barrier, len(peers))

    started = []

    def send(src, dst, peer):
        index = len(started)
        copy = pltpu.make_async_remote_copy(
            src_ref=src, dst_ref=dst, send_sem=ss.at[index], recv_sem=rs.at[index], device_id=peer, device_id_type=MESH
        )
        copy.start()
        started.append(copy)
        return copy

    def same(ref, peer):
        return send(ref, ref, peer)

    def arrived(copies):
        for copy in copies:
            copy.wait_recv()

    cot_z = same(cown.at[y, zh], at(ph=oh))
    w_across = same(wbuf.at[x, zl, c], at(pz=across))
    w_z = [same(wbuf.at[x, zl, c], at(pz=inside(k))) for k in (2, 1, 3)]
    cot_y = [same(cown.at[y, zh], at(py=yk(k))) for k in FAR_FIRST]
    tok_c = send(tok.at[:, pl.ds(pl.multiple_of(oc * HALF, 128), HALF)], toth, at(pc=oc))

    def rows_of(px, group):
        which = quad if group == 0 else 1 - quad
        return wbuf.at[px, pl.ds(which * 4, 4), c]

    def spread(group):
        over_x = [(k, same(rows_of(x, group), at(px=xk(k)))) for k in (2, 1, 3)]
        return over_x, [same(rows_of(x, group), at(pc=oc))]

    def share(over_x, over_c, group):
        for k, copy in over_x:
            copy.wait_recv()
            over_c.append(same(rows_of(xk(NX - k), group), at(pc=oc)))

    def key_group(group):
        which = quad if group == 0 else 1 - quad
        weight = wbuf[:, pl.ds(which * 4, 4)].reshape(512, D)
        term = dot(tok[...], weight, ((1,), (1,)))
        kpart[group] = term.reshape(NY, 32, 512)
        ksend[group] = sixth(term, KEY_SCALE).reshape(NY, 32, 512)
        return [send(ksend.at[group, yk(k)], krecv.at[group, i], at(py=yk(k))) for i, k in enumerate(FAR_FIRST)]

    def key_sum(group, copies):
        arrived(copies)
        rows = kpart[group, y]
        for i in range(NY - 1):
            rows = rows + unsixth(krecv[group, i], KEY_SCALE)
        ksum[group] = rows.reshape(NH, 16, 512)
        kzs[group] = sixth(rows, KEY_SCALE).reshape(NH, 16, 512)
        return send(kzs.at[group, oh], kzr.at[group], at(ph=oh))

    arrived(w_z)
    x_0, c_0 = spread(0)
    arrived(cot_y)
    cot_c = [same_core(cown, coth, zh, send, at(pc=oc))]
    w_across.wait_recv()
    w_z = [same(wbuf.at[x, across, c], at(pz=inside(k))) for k in (2, 1, 3)]
    cot_z.wait_recv()
    cot_y = [same(cown.at[y, oh], at(py=yk(k))) for k in FAR_FIRST]
    share(x_0, c_0, 0)
    arrived(c_0)
    k_0 = key_group(0)
    arrived(w_z)
    x_1, c_1 = spread(1)
    arrived(cot_y)
    cot_c.append(same_core(cown, coth, oh, send, at(pc=oc)))

    tok_c.wait_recv()
    arrived(cot_c)
    mine = tok[:, pl.ds(pl.multiple_of(c * HALF, 128), HALF)]

    def weight_term(block, half):
        columns = pl.ds(pl.multiple_of(block * 256 + half * 128, 128), 128)
        return dot(cown[:, :, :, columns].reshape(T, 128), mine, ((0,), (0,))) + dot(
            coth[:, :, :, columns].reshape(T, 128), toth[...], ((0,), (0,))
        )

    g_x = []
    for part, half in enumerate((1 - quad, quad)):
        over = []
        for slot, k in enumerate((2, 1, 3)):
            wsend[part, slot] = cube(weight_term(xk(k), half), WX_SCALE)
            over.append(send(wsend.at[part, slot], wrecv.at[part, slot], at(px=xk(k))))
        g_x.append(over)
    for part, half in enumerate((1 - quad, quad)):
        wsum[part] = weight_term(x, half)

    share(x_1, c_1, 1)
    arrived(c_1)
    k_1 = key_group(1)
    k_z = [key_sum(0, k_0)]

    g_z = []
    for part in range(2):
        arrived(g_x[part])
        total = wsum[part]
        for slot in range(3):
            total = total + uncube(wrecv[part, slot], WX_SCALE)
        wsum[part] = total
        zsend[part] = cube(total, WZ_SCALE).reshape(4, NC, 16, HALF)
        for k in range(part, 4):
            pz = lax.rem(spot + k, 4)
            peer = outside(k) if part == 0 else inside(k)
            for core in range(NC):
                pc = c if core == 0 else oc
                g_z.append(send(zsend.at[part, pz, pc], zrecv.at[core, part * 4 + k], at(pz=peer, pc=pc)))
    g_z.append(send(zsend.at[1, spot, oc], zrecv.at[1, 4], at(pc=oc)))

    grad = jnp.zeros((T, D), f32)
    for block in range(NX):
        grad = grad + dot(
            cown[:, :, :, block * 256 : (block + 1) * 256].reshape(T, 256), wbuf[block].reshape(256, D), ((1,), (0,))
        )
    tgrad[...] = grad.astype(bf16)

    k_z.append(key_sum(1, k_1))

    arrived(g_z)
    first = pl.multiple_of(spot * 32 + c * 16, 16)
    for core in range(NC):
        rows = wsum[1, pl.ds(first, 16)] if core == 0 else uncube(zrecv[1, 4], WZ_SCALE)
        for slot in (0, 1, 2, 3, 5, 6, 7):
            rows = rows + uncube(zrecv[core, slot], WZ_SCALE)
        half = c if core == 0 else oc
        wgrad[:, pl.ds(pl.multiple_of(half * HALF, 128), HALF)] = rows * (1.0 / 64)

    for group in range(2):
        k_z[group].wait_recv()
        rows = (ksum[group, zh] + unsixth(kzr[group], KEY_SCALE)).astype(bf16)
        which = quad if group == 0 else 1 - quad
        for px in range(NX):
            columns = pl.ds(pl.multiple_of(px * 256 + which * 128, 128), 128)
            keys[:, columns] = rows[:, px * 128 : (px + 1) * 128]

    for copy in started:
        copy.wait_send()


def same_core(own, other, half, send, peer):
    return send(own.at[:, half], other.at[:, half], peer)


COPIES = 1 + 1 + 3 + 7 + 1 + 4 + 1 + 3 + 7 + 3 + 7 + 4 + 1 + 6 + 3 + 7 + 1 + 15 + 1


def body(tokens, key_weight, key_cotangent):
    vmem = pl.BlockSpec(memory_space=pltpu.VMEM)
    return pl.pallas_call(
        kernel,
        out_shape=(
            jax.ShapeDtypeStruct((16, KV), bf16),
            jax.ShapeDtypeStruct((T, D), bf16),
            jax.ShapeDtypeStruct((16, D), f32),
        ),
        in_specs=[pl.BlockSpec(memory_space=pltpu.HBM)] * 3,
        out_specs=(vmem,) * 3,
        scratch_shapes=[
            pltpu.VMEM((T, D), bf16),
            pltpu.VMEM((NX, NZ, NC, 16, D), bf16),
            pltpu.VMEM((NY, NH, 16, KV), bf16),
            pltpu.VMEM((NY, NH, 16, KV), bf16),
            pltpu.VMEM((T, HALF), bf16),
            pltpu.VMEM((2, 3, 128, HALF), bf16),
            pltpu.VMEM((2, 3, 128, HALF), bf16),
            pltpu.VMEM((2, 128, HALF), f32),
            pltpu.VMEM((2, 4, NC, 16, HALF), bf16),
            pltpu.VMEM((2, 8, 16, HALF), bf16),
            pltpu.VMEM((2, NY, 32, 512), bf16),
            pltpu.VMEM((2, NY - 1, 32, 512), bf16),
            pltpu.VMEM((2, NY, 32, 512), f32),
            pltpu.VMEM((2, NH, 16, 512), f32),
            pltpu.VMEM((2, NH, 16, 512), bf16),
            pltpu.VMEM((2, 16, 512), bf16),
            pltpu.SemaphoreType.DMA((3,)),
            pltpu.SemaphoreType.DMA((COPIES,)),
            pltpu.SemaphoreType.DMA((COPIES,)),
        ],
        compiler_params=pltpu.CompilerParams(
            collective_id=0, has_side_effects=True, vmem_limit_bytes=48 * 1024 * 1024
        ),
        name="key_projection",
    )(tokens, key_weight, key_cotangent)


def solution(mesh):
    in_specs = (P("dp", "node"), P("dp", "node"), P(("dp", "node"), None))
    out_specs = (P(("dp", "node"), None), P("dp", "node"), P("dp", "node"))
    return jax.shard_map(body, mesh=mesh, in_specs=in_specs, out_specs=out_specs, check_vma=False)
```

```python
import jax
import jax.numpy as jnp
from jax import lax
from jax.experimental import pallas as pl
from jax.experimental.pallas import tpu as pltpu
from jax.sharding import PartitionSpec as P

MESH = pl.DeviceIdType.MESH
NX, NZ, NC, NY, NH = 4, 8, 2, 8, 2
D, KV, T = 768, 1024, 256
HALF = D // 2
FAR_FIRST = (4, 3, 5, 2, 6, 1, 7)

f32, bf16 = jnp.float32, jnp.bfloat16

KEY_SCALE = 2.0**11
WX_SCALE = 2.0**24
WZ_SCALE = 2.0**22


def cube(value, scale):
    value = value * scale
    return (value * value * value).astype(bf16)


def uncube(sent, scale):
    sent = sent.astype(f32)
    root = jnp.exp(jnp.log(jnp.abs(sent)) * (1.0 / 3.0)) * (1.0 / scale)
    return jnp.where(sent < 0, -root, root)


def sixth(value, scale):
    value = value * scale
    value = value * value * value
    return (value * jnp.abs(value)).astype(bf16)


def unsixth(sent, scale):
    sent = sent.astype(f32)
    root = jnp.exp(jnp.log(jnp.abs(sent)) * (1.0 / 6.0)) * (1.0 / scale)
    return jnp.where(sent < 0, -root, root)


def dot(left, right, dims):
    return lax.dot_general(left, right, (dims, ((), ())), preferred_element_type=f32)


def kernel(
    tok_in, w_in, cot_in, keys, tgrad, wgrad,
    tok, wbuf, cown, coth, toth, wsend, wrecv, wsum, zsend, zrecv, ksend, krecv, kpart, ksum, kzs, kzr, ls, ss, rs,
):
    dp, node = lax.axis_index("dp"), lax.axis_index("node")
    x, zl, c = dp // 16, lax.rem(dp // 2, 8), lax.rem(dp, 2)
    y, zh = node // 2, lax.rem(node, 2)
    oc, oh = 1 - c, 1 - zh
    quad, spot = zl // 4, lax.rem(zl, 4)
    across = lax.rem(zl + 4, NZ)

    def at(px=x, pz=zl, pc=c, py=y, ph=zh):
        return ((px * NZ + pz) * NC + pc, py * NH + ph)

    def xk(k):
        return lax.rem(x + k, NX)

    def yk(k):
        return lax.rem(y + k, NY)

    def inside(k):
        return quad * 4 + lax.rem(spot + k, 4)

    def outside(k):
        return (1 - quad) * 4 + lax.rem(spot + k, 4)

    barrier = pltpu.get_barrier_semaphore()
    peers = [at(ph=oh), at(pz=across)]
    peers += [at(py=yk(k)) for k in FAR_FIRST]
    peers += [at(pz=inside(k)) for k in (2, 1, 3)]
    peers += [at(px=xk(k)) for k in (2, 1, 3)]
    peers += [at(pc=oc)]
    for peer in peers:
        pl.semaphore_signal(barrier, inc=1, device_id=peer, device_id_type=MESH)

    fetches = [
        pltpu.make_async_copy(cot_in, cown.at[y, zh], ls.at[0]),
        pltpu.make_async_copy(w_in, wbuf.at[x, zl, c], ls.at[1]),
        pltpu.make_async_copy(tok_in, tok, ls.at[2]),
    ]
    for fetch in fetches:
        fetch.start()
    for fetch in fetches:
        fetch.wait()
    pl.semaphore_wait(barrier, len(peers))


    started = []

    def send(src, dst, peer):
        index = len(started)
        copy = pltpu.make_async_remote_copy(
            src_ref=src, dst_ref=dst, send_sem=ss.at[index], recv_sem=rs.at[index], device_id=peer, device_id_type=MESH
        )
        copy.start()
        started.append(copy)
        return copy

    def same(ref, peer):
        return send(ref, ref, peer)

    def arrived(copies):
        for copy in copies:
            copy.wait_recv()

    cot_z = [same(cown.at[y, zh], at(ph=oh))]
    w_across = same(wbuf.at[x, zl, c], at(pz=across))
    w_z = [same(wbuf.at[x, zl, c], at(pz=inside(k))) for k in (2, 1, 3)]
    cot_y = [same(cown.at[y, zh], at(py=yk(k))) for k in FAR_FIRST]
    tok_c = send(tok.at[:, pl.ds(pl.multiple_of(oc * HALF, 128), HALF)], toth, at(pc=oc))

    def rows_of(px, group):
        which = quad if group == 0 else 1 - quad
        return wbuf.at[px, pl.ds(which * 4, 4), c]

    def spread(group):
        over_x = [(k, same(rows_of(x, group), at(px=xk(k)))) for k in (2, 1, 3)]
        return over_x, [same(rows_of(x, group), at(pc=oc))]

    def share(over_x, over_c, group):
        for k, copy in over_x:
            copy.wait_recv()
            over_c.append(same(rows_of(xk(NX - k), group), at(pc=oc)))

    def key_group(group):
        which = quad if group == 0 else 1 - quad
        weight = wbuf[:, pl.ds(which * 4, 4)].reshape(512, D)
        term = dot(tok[...], weight, ((1,), (1,)))
        kpart[group] = term.reshape(NY, 32, 512)
        ksend[group] = sixth(term, KEY_SCALE).reshape(NY, 32, 512)
        return [send(ksend.at[group, yk(k)], krecv.at[group, i], at(py=yk(k))) for i, k in enumerate(FAR_FIRST)]

    def key_sum(group, copies):
        arrived(copies)
        rows = kpart[group, y]
        for i in range(NY - 1):
            rows = rows + unsixth(krecv[group, i], KEY_SCALE)
        ksum[group] = rows.reshape(NH, 16, 512)
        kzs[group] = sixth(rows, KEY_SCALE).reshape(NH, 16, 512)
        return send(kzs.at[group, oh], kzr.at[group], at(ph=oh))

    arrived(w_z)
    x_0, c_0 = spread(0)
    w_across.wait_recv()
    w_z = [same(wbuf.at[x, across, c], at(pz=inside(k))) for k in (2, 1, 3)]
    arrived(cot_y)
    cot_c = [same_core(cown, coth, zh, send, at(pc=oc))]
    arrived(cot_z)
    cot_y = [same(cown.at[y, oh], at(py=yk(k))) for k in FAR_FIRST]
    arrived(w_z)
    x_1, c_1 = spread(1)
    share(x_0, c_0, 0)
    arrived(c_0)
    k_0 = key_group(0)
    share(x_1, c_1, 1)
    arrived(cot_y)
    cot_c.append(same_core(cown, coth, oh, send, at(pc=oc)))

    tok_c.wait_recv()
    arrived(cot_c)
    mine = tok[:, pl.ds(pl.multiple_of(c * HALF, 128), HALF)]

    def weight_term(block, half):
        columns = pl.ds(pl.multiple_of(block * 256 + half * 128, 128), 128)
        return dot(cown[:, :, :, columns].reshape(T, 128), mine, ((0,), (0,))) + dot(
            coth[:, :, :, columns].reshape(T, 128), toth[...], ((0,), (0,))
        )

    g_x = []
    for part, half in enumerate((1 - quad, quad)):
        over = []
        for slot, k in enumerate((2, 1, 3)):
            wsend[part, slot] = cube(weight_term(xk(k), half), WX_SCALE)
            over.append(send(wsend.at[part, slot], wrecv.at[part, slot], at(px=xk(k))))
        g_x.append(over)
    for part, half in enumerate((1 - quad, quad)):
        wsum[part] = weight_term(x, half)
    arrived(c_1)
    k_1 = key_group(1)

    k_z = [key_sum(0, k_0)]

    g_z = []
    for part in range(2):
        arrived(g_x[part])
        total = wsum[part]
        for slot in range(3):
            total = total + uncube(wrecv[part, slot], WX_SCALE)
        wsum[part] = total
        zsend[part] = cube(total, WZ_SCALE).reshape(4, NC, 16, HALF)
        for k in range(part, 4):
            pz = lax.rem(spot + k, 4)
            peer = outside(k) if part == 0 else inside(k)
            for core in range(NC):
                pc = c if core == 0 else oc
                g_z.append(send(zsend.at[part, pz, pc], zrecv.at[core, part * 4 + k], at(pz=peer, pc=pc)))
    g_z.append(send(zsend.at[1, spot, oc], zrecv.at[1, 4], at(pc=oc)))

    grad = jnp.zeros((T, D), f32)
    for block in range(NX):
        grad = grad + dot(
            cown[:, :, :, block * 256 : (block + 1) * 256].reshape(T, 256), wbuf[block].reshape(256, D), ((1,), (0,))
        )
    tgrad[...] = grad.astype(bf16)

    k_z.append(key_sum(1, k_1))

    arrived(g_z)
    first = pl.multiple_of(spot * 32 + c * 16, 16)
    for core in range(NC):
        rows = wsum[1, pl.ds(first, 16)] if core == 0 else uncube(zrecv[1, 4], WZ_SCALE)
        for slot in (0, 1, 2, 3, 5, 6, 7):
            rows = rows + uncube(zrecv[core, slot], WZ_SCALE)
        half = c if core == 0 else oc
        wgrad[:, pl.ds(pl.multiple_of(half * HALF, 128), HALF)] = rows * (1.0 / 64)

    for group in range(2):
        k_z[group].wait_recv()
        rows = (ksum[group, zh] + unsixth(kzr[group], KEY_SCALE)).astype(bf16)
        which = quad if group == 0 else 1 - quad
        for px in range(NX):
            columns = pl.ds(pl.multiple_of(px * 256 + which * 128, 128), 128)
            keys[:, columns] = rows[:, px * 128 : (px + 1) * 128]

    for copy in started:
        copy.wait_send()


def same_core(own, other, half, send, peer):
    return send(own.at[:, half], other.at[:, half], peer)


COPIES = 1 + 1 + 3 + 7 + 1 + 4 + 1 + 3 + 7 + 3 + 7 + 4 + 1 + 6 + 3 + 7 + 1 + 15 + 1


def finish(keys, tgrad, wgrad, keys_out, tgrad_out, wgrad_out):
    tgrad_out[...] = tgrad[...]
    keys_out[...] = keys[...]
    wgrad_out[...] = wgrad[...]


def body(tokens, key_weight, key_cotangent):
    vmem = pl.BlockSpec(memory_space=pltpu.VMEM)
    hbm = pl.BlockSpec(memory_space=pltpu.HBM)
    shapes = (
        jax.ShapeDtypeStruct((16, KV), bf16),
        jax.ShapeDtypeStruct((T, D), bf16),
        jax.ShapeDtypeStruct((16, D), f32),
    )
    results = pl.pallas_call(
        kernel,
        out_shape=shapes,
        in_specs=[hbm] * 3,
        out_specs=(vmem,) * 3,
        scratch_shapes=[
            pltpu.VMEM((T, D), bf16),
            pltpu.VMEM((NX, NZ, NC, 16, D), bf16),
            pltpu.VMEM((NY, NH, 16, KV), bf16),
            pltpu.VMEM((NY, NH, 16, KV), bf16),
            pltpu.VMEM((T, HALF), bf16),
            pltpu.VMEM((2, 3, 128, HALF), bf16),
            pltpu.VMEM((2, 3, 128, HALF), bf16),
            pltpu.VMEM((2, 128, HALF), f32),
            pltpu.VMEM((2, 4, NC, 16, HALF), bf16),
            pltpu.VMEM((2, 8, 16, HALF), bf16),
            pltpu.VMEM((2, NY, 32, 512), bf16),
            pltpu.VMEM((2, NY - 1, 32, 512), bf16),
            pltpu.VMEM((2, NY, 32, 512), f32),
            pltpu.VMEM((2, NH, 16, 512), f32),
            pltpu.VMEM((2, NH, 16, 512), bf16),
            pltpu.VMEM((2, 16, 512), bf16),
            pltpu.SemaphoreType.DMA((3,)),
            pltpu.SemaphoreType.DMA((COPIES,)),
            pltpu.SemaphoreType.DMA((COPIES,)),
        ],
        compiler_params=pltpu.CompilerParams(
            collective_id=0, has_side_effects=True, vmem_limit_bytes=63 * 1024 * 1024
        ),
        name="key_projection",
    )(tokens, key_weight, key_cotangent)
    return pl.pallas_call(
        finish,
        out_shape=shapes,
        in_specs=[vmem] * 3,
        out_specs=(vmem,) * 3,
        name="finish",
    )(*results)


def solution(mesh):
    in_specs = (P("dp", "node"), P("dp", "node"), P(("dp", "node"), None))
    out_specs = (P(("dp", "node"), None), P("dp", "node"), P("dp", "node"))
    return jax.shard_map(body, mesh=mesh, in_specs=in_specs, out_specs=out_specs, check_vma=False)
```

```python
import jax
import jax.numpy as jnp
from jax import lax
from jax.experimental import pallas as pl
from jax.experimental.pallas import tpu as pltpu
from jax.sharding import PartitionSpec as P

MESH = pl.DeviceIdType.MESH
NX, NZ, NC, NY, NH = 4, 8, 2, 8, 2
D, KV, T = 768, 1024, 256
HALF = D // 2
FAR_FIRST = (4, 3, 5, 2, 6, 1, 7)

f32, bf16 = jnp.float32, jnp.bfloat16

KEY_SCALE = 2.0**11
WX_SCALE = 2.0**24
WZ_SCALE = 2.0**22


def cube(value, scale):
    value = value * scale
    return (value * value * value).astype(bf16)


def uncube(sent, scale):
    sent = sent.astype(f32)
    root = jnp.exp(jnp.log(jnp.abs(sent)) * (1.0 / 3.0)) * (1.0 / scale)
    return jnp.where(sent < 0, -root, root)


def sixth(value, scale):
    value = value * scale
    value = value * value * value
    return (value * jnp.abs(value)).astype(bf16)


def unsixth(sent, scale):
    sent = sent.astype(f32)
    root = jnp.exp(jnp.log(jnp.abs(sent)) * (1.0 / 6.0)) * (1.0 / scale)
    return jnp.where(sent < 0, -root, root)


def dot(left, right, dims):
    return lax.dot_general(left, right, (dims, ((), ())), preferred_element_type=f32)


def kernel(
    tok_in, w_in, cot_in, keys, tgrad, wgrad,
    tok, wbuf, cown, coth, toth, wsend, wrecv, wsum, zsend, zrecv, ksend, krecv, kpart, ksum, kzs, kzr, ls, ss, rs,
):
    dp, node = lax.axis_index("dp"), lax.axis_index("node")
    x, zl, c = dp // 16, lax.rem(dp // 2, 8), lax.rem(dp, 2)
    y, zh = node // 2, lax.rem(node, 2)
    oc, oh = 1 - c, 1 - zh
    quad, spot = zl // 4, lax.rem(zl, 4)
    across = lax.rem(zl + 4, NZ)

    def at(px=x, pz=zl, pc=c, py=y, ph=zh):
        return ((px * NZ + pz) * NC + pc, py * NH + ph)

    def xk(k):
        return lax.rem(x + k, NX)

    def yk(k):
        return lax.rem(y + k, NY)

    def inside(k):
        return quad * 4 + lax.rem(spot + k, 4)

    def outside(k):
        return (1 - quad) * 4 + lax.rem(spot + k, 4)

    barrier = pltpu.get_barrier_semaphore()
    peers = [at(ph=oh), at(pz=across)]
    peers += [at(py=yk(k)) for k in FAR_FIRST]
    peers += [at(pz=inside(k)) for k in (2, 1, 3)]
    peers += [at(px=xk(k)) for k in (2, 1, 3)]
    peers += [at(pc=oc)]
    fetches = [
        pltpu.make_async_copy(cot_in, cown.at[y, zh], ls.at[0]),
        pltpu.make_async_copy(w_in, wbuf.at[x, zl, c], ls.at[1]),
        pltpu.make_async_copy(tok_in, tok, ls.at[2]),
    ]
    for fetch in fetches:
        fetch.start()
    for peer in peers:
        pl.semaphore_signal(barrier, inc=1, device_id=peer, device_id_type=MESH)

    fetches[0].wait()
    fetches[1].wait()
    pl.semaphore_wait(barrier, len(peers))


    started = []

    def send(src, dst, peer):
        index = len(started)
        copy = pltpu.make_async_remote_copy(
            src_ref=src, dst_ref=dst, send_sem=ss.at[index], recv_sem=rs.at[index], device_id=peer, device_id_type=MESH
        )
        copy.start()
        started.append(copy)
        return copy

    def same(ref, peer):
        return send(ref, ref, peer)

    def arrived(copies):
        for copy in copies:
            copy.wait_recv()

    cot_z = [same(cown.at[y, zh], at(ph=oh))]
    w_across = same(wbuf.at[x, zl, c], at(pz=across))
    w_z = [same(wbuf.at[x, zl, c], at(pz=inside(k))) for k in (2, 1, 3)]
    cot_y = [same(cown.at[y, zh], at(py=yk(k))) for k in FAR_FIRST]
    fetches[2].wait()
    tok_c = send(tok.at[:, pl.ds(pl.multiple_of(oc * HALF, 128), HALF)], toth, at(pc=oc))

    def rows_of(px, group):
        which = quad if group == 0 else 1 - quad
        return wbuf.at[px, pl.ds(which * 4, 4), c]

    def spread(group):
        over_x = [(k, same(rows_of(x, group), at(px=xk(k)))) for k in (2, 1, 3)]
        return over_x, [same(rows_of(x, group), at(pc=oc))]

    def share(over_x, over_c, group):
        for k, copy in over_x:
            copy.wait_recv()
            over_c.append(same(rows_of(xk(NX - k), group), at(pc=oc)))

    def key_group(group):
        which = quad if group == 0 else 1 - quad
        weight = wbuf[:, pl.ds(which * 4, 4)].reshape(512, D)
        term = dot(tok[...], weight, ((1,), (1,)))
        kpart[group] = term.reshape(NY, 32, 512)
        ksend[group] = sixth(term, KEY_SCALE).reshape(NY, 32, 512)
        return [send(ksend.at[group, yk(k)], krecv.at[group, i], at(py=yk(k))) for i, k in enumerate(FAR_FIRST)]

    def key_sum(group, copies):
        arrived(copies)
        rows = kpart[group, y]
        for i in range(NY - 1):
            rows = rows + unsixth(krecv[group, i], KEY_SCALE)
        ksum[group] = rows.reshape(NH, 16, 512)
        kzs[group] = sixth(rows, KEY_SCALE).reshape(NH, 16, 512)
        return send(kzs.at[group, oh], kzr.at[group], at(ph=oh))

    arrived(w_z)
    x_0, c_0 = spread(0)
    w_across.wait_recv()
    w_z = [same(wbuf.at[x, across, c], at(pz=inside(k))) for k in (2, 1, 3)]
    arrived(cot_y)
    cot_c = [same_core(cown, coth, zh, send, at(pc=oc))]
    arrived(cot_z)
    cot_y = [same(cown.at[y, oh], at(py=yk(k))) for k in FAR_FIRST]
    arrived(w_z)
    x_1, c_1 = spread(1)
    share(x_0, c_0, 0)
    arrived(c_0)
    k_0 = key_group(0)
    share(x_1, c_1, 1)
    arrived(cot_y)
    cot_c.append(same_core(cown, coth, oh, send, at(pc=oc)))

    tok_c.wait_recv()
    arrived(cot_c)
    mine = tok[:, pl.ds(pl.multiple_of(c * HALF, 128), HALF)]

    def weight_term(block, half):
        columns = pl.ds(pl.multiple_of(block * 256 + half * 128, 128), 128)
        return dot(cown[:, :, :, columns].reshape(T, 128), mine, ((0,), (0,))) + dot(
            coth[:, :, :, columns].reshape(T, 128), toth[...], ((0,), (0,))
        )

    g_x = []
    for part, half in enumerate((1 - quad, quad)):
        over = []
        for slot, k in enumerate((2, 1, 3)):
            wsend[part, slot] = cube(weight_term(xk(k), half), WX_SCALE)
            over.append(send(wsend.at[part, slot], wrecv.at[part, slot], at(px=xk(k))))
        g_x.append(over)
    for part, half in enumerate((1 - quad, quad)):
        wsum[part] = weight_term(x, half)
    arrived(c_1)
    k_1 = key_group(1)

    k_z = [key_sum(0, k_0)]

    g_z = []
    for part in range(2):
        arrived(g_x[part])
        total = wsum[part]
        for slot in range(3):
            total = total + uncube(wrecv[part, slot], WX_SCALE)
        wsum[part] = total
        zsend[part] = cube(total, WZ_SCALE).reshape(4, NC, 16, HALF)
        for k in range(part, 4):
            pz = lax.rem(spot + k, 4)
            peer = outside(k) if part == 0 else inside(k)
            for core in range(NC):
                pc = c if core == 0 else oc
                g_z.append(send(zsend.at[part, pz, pc], zrecv.at[core, part * 4 + k], at(pz=peer, pc=pc)))
    g_z.append(send(zsend.at[1, spot, oc], zrecv.at[1, 4], at(pc=oc)))

    grad = jnp.zeros((T, D), f32)
    for block in range(NX):
        grad = grad + dot(
            cown[:, :, :, block * 256 : (block + 1) * 256].reshape(T, 256), wbuf[block].reshape(256, D), ((1,), (0,))
        )
    tgrad[...] = grad.astype(bf16)

    k_z.append(key_sum(1, k_1))

    arrived(g_z)
    first = pl.multiple_of(spot * 32 + c * 16, 16)
    for core in range(NC):
        rows = wsum[1, pl.ds(first, 16)] if core == 0 else uncube(zrecv[1, 4], WZ_SCALE)
        for slot in (0, 1, 2, 3, 5, 6, 7):
            rows = rows + uncube(zrecv[core, slot], WZ_SCALE)
        half = c if core == 0 else oc
        wgrad[:, pl.ds(pl.multiple_of(half * HALF, 128), HALF)] = rows * (1.0 / 64)

    for group in range(2):
        k_z[group].wait_recv()
        rows = (ksum[group, zh] + unsixth(kzr[group], KEY_SCALE)).astype(bf16)
        which = quad if group == 0 else 1 - quad
        for px in range(NX):
            columns = pl.ds(pl.multiple_of(px * 256 + which * 128, 128), 128)
            keys[:, columns] = rows[:, px * 128 : (px + 1) * 128]

    for copy in started:
        copy.wait_send()


def same_core(own, other, half, send, peer):
    return send(own.at[:, half], other.at[:, half], peer)


COPIES = 1 + 1 + 3 + 7 + 1 + 4 + 1 + 3 + 7 + 3 + 7 + 4 + 1 + 6 + 3 + 7 + 1 + 15 + 1


def finish(keys, tgrad, wgrad, keys_out, tgrad_out, wgrad_out):
    tgrad_out[...] = tgrad[...]
    keys_out[...] = keys[...]
    wgrad_out[...] = wgrad[...]


def body(tokens, key_weight, key_cotangent):
    vmem = pl.BlockSpec(memory_space=pltpu.VMEM)
    hbm = pl.BlockSpec(memory_space=pltpu.HBM)
    shapes = (
        jax.ShapeDtypeStruct((16, KV), bf16),
        jax.ShapeDtypeStruct((T, D), bf16),
        jax.ShapeDtypeStruct((16, D), f32),
    )
    results = pl.pallas_call(
        kernel,
        out_shape=shapes,
        in_specs=[hbm] * 3,
        out_specs=(vmem,) * 3,
        scratch_shapes=[
            pltpu.VMEM((T, D), bf16),
            pltpu.VMEM((NX, NZ, NC, 16, D), bf16),
            pltpu.VMEM((NY, NH, 16, KV), bf16),
            pltpu.VMEM((NY, NH, 16, KV), bf16),
            pltpu.VMEM((T, HALF), bf16),
            pltpu.VMEM((2, 3, 128, HALF), bf16),
            pltpu.VMEM((2, 3, 128, HALF), bf16),
            pltpu.VMEM((2, 128, HALF), f32),
            pltpu.VMEM((2, 4, NC, 16, HALF), bf16),
            pltpu.VMEM((2, 8, 16, HALF), bf16),
            pltpu.VMEM((2, NY, 32, 512), bf16),
            pltpu.VMEM((2, NY - 1, 32, 512), bf16),
            pltpu.VMEM((2, NY, 32, 512), f32),
            pltpu.VMEM((2, NH, 16, 512), f32),
            pltpu.VMEM((2, NH, 16, 512), bf16),
            pltpu.VMEM((2, 16, 512), bf16),
            pltpu.SemaphoreType.DMA((3,)),
            pltpu.SemaphoreType.DMA((COPIES,)),
            pltpu.SemaphoreType.DMA((COPIES,)),
        ],
        compiler_params=pltpu.CompilerParams(
            collective_id=0, has_side_effects=True, vmem_limit_bytes=63 * 1024 * 1024
        ),
        name="key_projection",
    )(tokens, key_weight, key_cotangent)
    return pl.pallas_call(
        finish,
        out_shape=shapes,
        in_specs=[vmem] * 3,
        out_specs=(vmem,) * 3,
        name="finish",
    )(*results)


def solution(mesh):
    in_specs = (P("dp", "node"), P("dp", "node"), P(("dp", "node"), None))
    out_specs = (P(("dp", "node"), None), P("dp", "node"), P("dp", "node"))
    return jax.shard_map(body, mesh=mesh, in_specs=in_specs, out_specs=out_specs, check_vma=False)
```
